512 devices in a mesh: rep: 8 (over y, x_hi), fsdp: 64 (over z, x_lo, core).
Axes of the slice: x: 4 (x_hi: 2, x_lo: 2; x = x_hi * 2 + x_lo), y: 4, z: 16, core: 2. Of those that a mesh axis runs over, the one named last changes fastest.
Arguments:
- activations: bfloat16 [8, 40960, 3072], P('rep', 'fsdp'), may hold values from -16 to 16
- cotangent: bfloat16 [8, 40960, 256], P('rep', 'fsdp'), may hold values from -0.03125 to 0.03125
- momentum: float32 [8, 3072, 256], P('rep', 'fsdp'), may hold values from -6 to 6
- components: int32 [8, 3072, 4, 8], P('rep', 'fsdp'), may hold values from 0 to 63, as said below
Outputs:
- update: float32 [3072, 256], P('fsdp')
- renewed: float32 [8, 3072, 256], P('rep', 'fsdp')
The draws below stay inside these ranges and needn't reach their ends.
Inputs may be any that keep to these rules, and one draw needn't show every extreme that they name: The 8 components listed for one span are distinct.
All inputs are finite; a program needn't handle non-finite values.
Results may differ from the reference program's by a relative error of at most 0.0003.
Values sent between devices are 32-bit elements; how exact they have to be, the bound alone decides.
No kernel may reach another device: no remote copies, remote signals or barrier semaphores. Data moves between devices by JAX's collectives and lax.ppermute only.
A program may use at most 64 MiB of HBM per device.

```python
import math
import jax
import jax.numpy as jnp
from jax import lax

D = 3072
KV = 256
SPAN = 64
TOPK = 8
TOK_DEV = 640
TOKENS = 40960
N_REP = 8
N_FSDP = 64


def draw_components(key, part):
    key = jax.random.fold_in(key, 5)
    scores = jax.random.randint(key, (N_REP, D, KV // SPAN, SPAN), 0, 1 << 20) * SPAN
    scores = scores + jnp.arange(SPAN, dtype=jnp.int32)
    _, chosen = lax.top_k(scores, TOPK)
    return chosen.astype(jnp.int32)


def with_spikes(entries, stream_key, source, target, blocks, factor):
    def block_of(dim):
        return (jnp.arange(entries.shape[dim]) // (entries.shape[dim] // blocks)).reshape((-1,) + (1,) * (entries.ndim - 1 - dim))

    first = jax.random.permutation(stream_key, blocks)[block_of(target)]
    other_side = (block_of(target) + blocks // 2) % blocks
    return jnp.where((block_of(source) == first) | (block_of(source) == other_side), factor * entries, entries)


def block_levels(rng, extent, pieces, least, largest):
    factor_of, own = 1.0, jax.random.fold_in(rng, 6)
    for axis_at, parts in pieces:
        heights = jnp.exp(jax.random.uniform(jax.random.fold_in(own, axis_at), (parts,), jnp.float32, least / len(pieces), largest / len(pieces)))
        factor_of = factor_of * jnp.repeat(heights, extent[axis_at] // parts).reshape([-1 if axis == axis_at else 1 for axis in range(len(extent))])
    return factor_of


def bell_draw(stream_key, extent, deviation, bound, split=(), held_as=jnp.bfloat16):
    level = block_levels(stream_key, extent, split, -0.22, 0.18) if split else 1.0
    drawn = jax.random.normal(stream_key, extent, jnp.float32) * deviation * level
    return jnp.minimum(jnp.maximum(drawn, -bound), bound).astype(held_as)


def bell_draw_with(stream_key, extent, scale, bound, pieces, heavy, kind=jnp.bfloat16):
    array = scale * jax.random.normal(stream_key, extent, jnp.float32)
    if pieces:
        array = array * block_levels(stream_key, extent, pieces, -0.22, 0.18)
    return jnp.clip(with_spikes(array, jax.random.fold_in(stream_key, 3), *heavy), -bound, bound).astype(kind)


def setup_inputs(seed: int = 0) -> dict:
    keys = jax.random.split(jax.random.key(seed), 5)
    return {
        "activations": bell_draw_with(keys[0], (N_REP, TOKENS, D), 1.0, 16.0, ((0, 8), (1, 64)), (1, 2, 64, 4.0)),
        "cotangent": bell_draw(keys[1], (N_REP, TOKENS, KV), TOKENS ** -0.5, 0.03125, ((0, 8), (1, 64))),
        "momentum": bell_draw(keys[2], (N_REP, D, KV), 1.0, 6.0, ((0, 8), (1, 64)), jnp.float32),
        "components": draw_components(jax.random.fold_in(keys[4], 71), 0),
    }


beta_decay = 0.999
highest = lax.Precision.HIGHEST

def dct_table(length_span):
    frequency = jnp.arange(length_span, dtype=jnp.float32)[:, None]
    position = jnp.arange(length_span, dtype=jnp.float32)[None, :]
    cosine_raw = jnp.cos(math.pi * (2.0 * position + 1.0) * frequency / (2.0 * length_span))
    normalizer = jnp.where(frequency == 0.0, math.sqrt(1.0 / length_span), math.sqrt(2.0 / length_span))
    return (cosine_raw * normalizer).astype(jnp.float32)

def reference(activations, cotangent, momentum, components):
    cosines = dct_table(SPAN)

    def group_gradient(pair_in):
        act_blocks = pair_in[0].reshape(N_FSDP, TOK_DEV, D)
        cot_blocks = pair_in[1].reshape(N_FSDP, TOK_DEV, KV)

        def add_block(total, block_pair):
            partial_value = jnp.dot(block_pair[0].T, block_pair[1], preferred_element_type=jnp.float32)
            return (total + partial_value, None)
        total, _ = lax.scan(add_block, jnp.zeros((D, KV), jnp.float32), (act_blocks, cot_blocks))
        return total
    gradient = lax.map(group_gradient, (activations, cotangent))
    moment_new = beta_decay * momentum + gradient
    spans = moment_new.reshape(N_REP, D, KV // SPAN, SPAN)
    spectrum = jnp.einsum('grcn,kn->grck', spans, cosines, precision=highest)
    onehot = (components[..., None] == jnp.arange(SPAN, dtype=jnp.int32)).astype(jnp.float32)
    amounts = jnp.einsum('grcjk,grck->grcj', onehot, spectrum, precision=highest)
    retained = jnp.einsum('grcjk,grcj->grck', onehot, amounts, precision=highest)
    restored = jnp.einsum('grck,kn->grcn', retained, cosines, precision=highest).reshape(N_REP, D, KV)
    renewed = moment_new - restored
    summed = lax.optimization_barrier(jnp.sum(retained, axis=0))
    update = jnp.einsum('rck,kn->rcn', summed, cosines, precision=highest).reshape(D, KV) / N_REP
    return (update, renewed)
```

```python
import math

import jax
import jax.numpy as jnp
import numpy as np
from jax import lax
from jax.experimental import pallas as pl
from jax.experimental.pallas import tpu as pltpu
from jax.sharding import PartitionSpec as P

SPAN = 64
PAIRS = 8
beta_decay = 0.999
highest = lax.Precision.HIGHEST


def span_tables(cols):
    frequency = np.arange(SPAN, dtype=np.float64)[:, None]
    position = np.arange(SPAN, dtype=np.float64)[None, :]
    cosines = np.cos(math.pi * (2.0 * position + 1.0) * frequency / (2.0 * SPAN))
    cosines *= np.where(frequency == 0.0, math.sqrt(1.0 / SPAN), math.sqrt(2.0 / SPAN))
    return np.kron(np.eye(cols // SPAN), cosines.T).astype(np.float32)


def place(index):
    z = index // 4
    pair, bit = z // 2, z % 2
    return pair, bit ^ (pair // 4), (index // 2) % 2, index % 2


def index_of(pair, group, x, core):
    return (2 * pair + (group ^ (pair // 4))) * 4 + x * 2 + core


def swapped(dgroup, dx, dcore):
    pairs = []
    for f in range(64):
        pair, group, x, core = place(f)
        pairs.append((f, index_of(pair, group ^ dgroup, x ^ dx, core ^ dcore)))
    return pairs


def partial_kernel(acts_ref, cot_ref, out_ref):
    step = pl.program_id(0)
    _, group, x, core = place(lax.axis_index("fsdp"))
    product = lax.dot_general(
        acts_ref[...], cot_ref[...], (((0,), (0,)), ((), ())), preferred_element_type=jnp.float32
    )
    rows = product.shape[0] // 8
    for bit in range(2):
        for to_x in range(2):
            for to_core in range(2):
                at = (bit * 4 + to_x * 2 + to_core) * rows
                out_ref[to_core ^ core, bit ^ (step // 4) ^ group, to_x ^ x, 0] = product[at : at + rows]


def partials(acts, cot):
    tokens, dim = acts.shape
    cols = cot.shape[1]
    width = dim // PAIRS
    return pl.pallas_call(
        partial_kernel,
        grid=(PAIRS,),
        in_specs=[
            pl.BlockSpec((tokens, width), lambda p: (0, p)),
            pl.BlockSpec((tokens, cols), lambda p: (0, 0)),
        ],
        out_specs=pl.BlockSpec((2, 2, 2, 1, width // 8, cols), lambda p: (0, 0, 0, p, 0, 0)),
        out_shape=jax.ShapeDtypeStruct((2, 2, 2, PAIRS, width // 8, cols), jnp.float32),
        compiler_params=pltpu.CompilerParams(vmem_limit_bytes=48 << 20),
    )(acts, cot)


def encode_kernel(pieces_ref, moment_ref, chosen_ref, table_ref, renewed_ref, copies_ref):
    moment_new = beta_decay * moment_ref[...] + jnp.sum(pieces_ref[...], axis=0)
    rows, cols = moment_new.shape
    spans, kept, _ = chosen_ref.shape
    spectrum = jnp.dot(moment_new, table_ref[...], precision=highest, preferred_element_type=jnp.float32)
    component = lax.broadcasted_iota(jnp.int32, (SPAN, rows), 0)
    masks = []
    for c in range(spans):
        hit = component == chosen_ref[c, 0:1, :]
        for j in range(1, kept):
            hit = hit | (component == chosen_ref[c, j : j + 1, :])
        masks.append(jnp.where(hit, 1.0, 0.0))
    mask = jnp.concatenate(masks, axis=0).T
    retained = jnp.where(mask > 0.5, spectrum, 0.0)
    restored = lax.dot_general(
        retained, table_ref[...], (((1,), (1,)), ((), ())), precision=highest, preferred_element_type=jnp.float32
    )
    renewed_ref[...] = moment_new - restored
    copies_ref[...] = jnp.broadcast_to(restored, copies_ref.shape)


def encode(pieces, moment, chosen, copies):
    rows, cols = moment.shape
    return pl.pallas_call(
        encode_kernel,
        out_shape=(
            jax.ShapeDtypeStruct((rows, cols), jnp.float32),
            jax.ShapeDtypeStruct((copies, rows, cols), jnp.float32),
        ),
    )(pieces, moment, chosen, jnp.asarray(span_tables(cols)))


def shards(activations, cotangent, momentum, components):
    groups = lax.axis_size("rep")
    part = partials(activations[0], cotangent[0])
    mine = part[0] + lax.ppermute(part[1], "fsdp", swapped(0, 0, 1))
    both = lax.ppermute(mine[1, 1], "fsdp", swapped(1, 1, 0))
    along_x = lax.ppermute(mine[0, 1], "fsdp", swapped(0, 1, 0))
    along_z = lax.ppermute(mine[1, 0], "fsdp", swapped(1, 0, 0))
    mine = mine[0, 0] + both + along_x + along_z
    members = [
        [index_of(pair, group, x, core) for pair in range(PAIRS)]
        for group in range(2)
        for x in range(2)
        for core in range(2)
    ]
    pieces = lax.all_to_all(mine, "fsdp", 0, 0, axis_index_groups=members)
    chosen = components[0].transpose(1, 2, 0)
    renewed, copies = encode(pieces, momentum[0], chosen, groups)
    restored = lax.all_to_all(copies, "rep", 0, 0)
    update = jnp.sum(restored, axis=0) / groups
    return (update, renewed[None])


def solution(mesh):
    return jax.shard_map(
        shards,
        mesh=mesh,
        in_specs=(
            P("rep", "fsdp", None),
            P("rep", "fsdp", None),
            P("rep", "fsdp", None),
            P("rep", "fsdp", None, None),
        ),
        out_specs=(P("fsdp", None), P("rep", "fsdp", None)),
        check_vma=False,
    )
```

```python
import math

import jax
import jax.numpy as jnp
import numpy as np
from jax import lax
from jax.experimental import pallas as pl
from jax.experimental.pallas import tpu as pltpu
from jax.sharding import PartitionSpec as P

SPAN = 64
PAIRS = 8
beta_decay = 0.999
highest = lax.Precision.HIGHEST


def span_tables(cols):
    frequency = np.arange(SPAN, dtype=np.float64)[:, None]
    position = np.arange(SPAN, dtype=np.float64)[None, :]
    cosines = np.cos(math.pi * (2.0 * position + 1.0) * frequency / (2.0 * SPAN))
    cosines *= np.where(frequency == 0.0, math.sqrt(1.0 / SPAN), math.sqrt(2.0 / SPAN))
    return np.kron(np.eye(cols // SPAN), cosines.T).astype(np.float32)


def place(index):
    z = index // 4
    pair, bit = z // 2, z % 2
    return pair, bit ^ (pair // 4), (index // 2) % 2, index % 2


def index_of(pair, group, x, core):
    return (2 * pair + (group ^ (pair // 4))) * 4 + x * 2 + core


def swapped(dgroup, dx, dcore):
    pairs = []
    for f in range(64):
        pair, group, x, core = place(f)
        pairs.append((f, index_of(pair, group ^ dgroup, x ^ dx, core ^ dcore)))
    return pairs


def in_hbm(array):
    return pltpu.with_memory_space_constraint(array, pltpu.HBM)


def partial_kernel(
    acts_hbm, cot_hbm, chosen_hbm, out_ref, mask_ref, acts, cot, chosen_ref, acts_sem, cot_sem, chosen_sem
):
    copy_chosen = pltpu.make_async_copy(chosen_hbm, chosen_ref, chosen_sem)
    copy_chosen.start()
    copy_cot = pltpu.make_async_copy(cot_hbm, cot, cot_sem)
    copy_cot.start()
    copy_acts = pltpu.make_async_copy(acts_hbm, acts, acts_sem)
    copy_acts.start()
    spans, kept, rows = chosen_ref.shape
    copy_chosen.wait()
    component = lax.broadcasted_iota(jnp.int32, (SPAN, rows), 0)
    masks = []
    for c in range(spans):
        hit = component == chosen_ref[c, 0:1, :]
        for j in range(1, kept):
            hit = hit | (component == chosen_ref[c, j : j + 1, :])
        masks.append(jnp.where(hit, 1.0, 0.0))
    mask_ref[...] = jnp.concatenate(masks, axis=0).T
    _, group, x, core = place(lax.axis_index("fsdp"))
    copy_cot.wait()
    turned = cot[...].T
    copy_acts.wait()
    width = acts.shape[1] // 4
    for step in range(4):
        product = jnp.dot(
            turned, acts[:, step * width : (step + 1) * width], preferred_element_type=jnp.float32
        ).T
        for at in range(0, width, rows):
            pair, bit, to_x, to_core = place((step * width + at) // rows)
            out_ref[to_core ^ core, pair // 4, to_x ^ x, bit ^ group, pair % 4] = product[at : at + rows]


def partials(acts, cot, chosen):
    dim, cols = acts.shape[1], cot.shape[1]
    rows = chosen.shape[2]
    return pl.pallas_call(
        partial_kernel,
        in_specs=[
            pl.BlockSpec(memory_space=pl.ANY),
            pl.BlockSpec(memory_space=pl.ANY),
            pl.BlockSpec(memory_space=pl.ANY),
        ],
        out_shape=(
            jax.ShapeDtypeStruct((2, 2, 2, 2, PAIRS // 2, dim // (8 * PAIRS), cols), jnp.float32),
            jax.ShapeDtypeStruct((rows, cols), jnp.float32),
        ),
        scratch_shapes=[
            pltpu.VMEM(acts.shape, acts.dtype),
            pltpu.VMEM(cot.shape, cot.dtype),
            pltpu.VMEM(chosen.shape, chosen.dtype),
            pltpu.SemaphoreType.DMA,
            pltpu.SemaphoreType.DMA,
            pltpu.SemaphoreType.DMA,
        ],
        compiler_params=pltpu.CompilerParams(vmem_limit_bytes=40 << 20),
    )(in_hbm(acts), in_hbm(cot), in_hbm(chosen))


def encode_kernel(pieces_ref, moment_ref, mask_ref, table_ref, renewed_ref, copies_ref):
    moment_new = beta_decay * moment_ref[...] + jnp.sum(pieces_ref[...], axis=0)
    spectrum = jnp.dot(moment_new, table_ref[...], precision=highest, preferred_element_type=jnp.float32)
    retained = jnp.where(mask_ref[...] > 0.5, spectrum, 0.0)
    restored = lax.dot_general(
        retained, table_ref[...], (((1,), (1,)), ((), ())), precision=highest, preferred_element_type=jnp.float32
    )
    renewed_ref[...] = moment_new - restored
    copies_ref[...] = jnp.broadcast_to(restored, copies_ref.shape)


def encode(pieces, moment, mask, copies):
    rows, cols = moment.shape
    return pl.pallas_call(
        encode_kernel,
        out_shape=(
            jax.ShapeDtypeStruct((rows, cols), jnp.float32),
            jax.ShapeDtypeStruct((copies, rows, cols), jnp.float32),
        ),
    )(pieces, moment, mask, jnp.asarray(span_tables(cols)))


def shards(activations, cotangent, momentum, components):
    groups = lax.axis_size("rep")
    part, mask = partials(activations[0], cotangent[0], components[0].transpose(1, 2, 0))
    first = part[0, 0] + lax.ppermute(part[1, 0], "fsdp", swapped(0, 0, 1))
    second = part[0, 1] + lax.ppermute(part[1, 1], "fsdp", swapped(0, 0, 1))
    first = first[0] + lax.ppermute(first[1], "fsdp", swapped(0, 1, 0))
    second = second[:, 0] + lax.ppermute(second[:, 1], "fsdp", swapped(1, 0, 0))
    first = first[0] + lax.ppermute(first[1], "fsdp", swapped(1, 0, 0))
    second = second[0] + lax.ppermute(second[1], "fsdp", swapped(0, 1, 0))
    mine = jnp.concatenate([first, second])
    members = [
        [index_of(pair, group, x, core) for pair in range(PAIRS)]
        for group in range(2)
        for x in range(2)
        for core in range(2)
    ]
    pieces = lax.all_to_all(mine, "fsdp", 0, 0, axis_index_groups=members)
    renewed, copies = encode(pieces, momentum[0], mask, groups)
    restored = lax.all_to_all(copies, "rep", 0, 0)
    update = jnp.sum(restored, axis=0) / groups
    return (update, renewed[None])


def solution(mesh):
    return jax.shard_map(
        shards,
        mesh=mesh,
        in_specs=(
            P("rep", "fsdp", None),
            P("rep", "fsdp", None),
            P("rep", "fsdp", None),
            P("rep", "fsdp", None, None),
        ),
        out_specs=(P("fsdp", None), P("rep", "fsdp", None)),
        check_vma=False,
    )
```

```python
import math

import jax
import jax.numpy as jnp
import numpy as np
from jax import lax
from jax.experimental import pallas as pl
from jax.experimental.pallas import tpu as pltpu
from jax.sharding import PartitionSpec as P

SPAN = 64
PAIRS = 8
beta_decay = 0.999
highest = lax.Precision.HIGHEST


def span_tables(cols):
    frequency = np.arange(SPAN, dtype=np.float64)[:, None]
    position = np.arange(SPAN, dtype=np.float64)[None, :]
    cosines = np.cos(math.pi * (2.0 * position + 1.0) * frequency / (2.0 * SPAN))
    cosines *= np.where(frequency == 0.0, math.sqrt(1.0 / SPAN), math.sqrt(2.0 / SPAN))
    return np.kron(np.eye(cols // SPAN), cosines.T).astype(np.float32)


def place(index):
    z = index // 4
    pair, bit = z // 2, z % 2
    return pair, bit ^ (pair // 4), (index // 2) % 2, index % 2


def index_of(pair, group, x, core):
    return (2 * pair + (group ^ (pair // 4))) * 4 + x * 2 + core


def partners(of):
    pairs = []
    for f in range(64):
        pair, group, x, core = place(f)
        dgroup, dx, dcore = of(core)
        pairs.append((f, index_of(pair, group ^ dgroup, x ^ dx, core ^ dcore)))
    return pairs


def in_hbm(array):
    return pltpu.with_memory_space_constraint(array, pltpu.HBM)


def partial_kernel(
    acts_hbm, cot_hbm, chosen_hbm, away_ref, near_ref, keep_away_ref, keep_near_ref, mask_ref, product, acts, cot, chosen_ref, acts_sem, cot_sem, chosen_sem
):
    copy_chosen = pltpu.make_async_copy(chosen_hbm, chosen_ref, chosen_sem)
    copy_chosen.start()
    copy_cot = pltpu.make_async_copy(cot_hbm, cot, cot_sem)
    copy_cot.start()
    copy_acts = pltpu.make_async_copy(acts_hbm, acts, acts_sem)
    copy_acts.start()
    spans, kept, rows = chosen_ref.shape
    copy_chosen.wait()
    component = lax.broadcasted_iota(jnp.int32, (SPAN, rows), 0)
    masks = []
    for c in range(spans):
        hit = component == chosen_ref[c, 0:1, :]
        for j in range(1, kept):
            hit = hit | (component == chosen_ref[c, j : j + 1, :])
        masks.append(jnp.where(hit, 1.0, 0.0))
    mask_ref[...] = jnp.concatenate(masks, axis=0).T
    send_refs, keep_refs = (away_ref, near_ref), (keep_away_ref, keep_near_ref)
    _, group, x, core = place(lax.axis_index("fsdp"))
    copy_cot.wait()
    turned = cot[...].T
    copy_acts.wait()
    width = acts.shape[1] // 4
    for step in range(4):
        product[...] = jnp.dot(
            turned, acts[:, step * width : (step + 1) * width], preferred_element_type=jnp.float32
        ).T
        for local in range(width // (8 * rows)):
            pair = step * (width // (8 * rows)) + local
            for slot in range(4):
                early, late = 1 - slot // 2, 1 - slot % 2
                for to_core, at_core in ((core, keep_refs), (1 - core, send_refs)):
                    to_x = jnp.where(to_core == 0, early, late) ^ x
                    bit = jnp.where(to_core == 0, late, early) ^ group ^ (pair // 4)
                    at = (((local * 2 + bit) * 2 + to_x) * 2 + to_core) * rows
                    at_core[slot // 2][slot % 2, pair] = product[pl.ds(pl.multiple_of(at, 8), rows)]


def partials(acts, cot, chosen):
    dim, cols = acts.shape[1], cot.shape[1]
    rows = chosen.shape[2]
    return pl.pallas_call(
        partial_kernel,
        in_specs=[
            pl.BlockSpec(memory_space=pl.ANY),
            pl.BlockSpec(memory_space=pl.ANY),
            pl.BlockSpec(memory_space=pl.ANY),
        ],
        out_shape=(
            jax.ShapeDtypeStruct((2, PAIRS, rows, cols), jnp.float32),
            jax.ShapeDtypeStruct((2, PAIRS, rows, cols), jnp.float32),
            jax.ShapeDtypeStruct((2, PAIRS, rows, cols), jnp.float32),
            jax.ShapeDtypeStruct((2, PAIRS, rows, cols), jnp.float32),
            jax.ShapeDtypeStruct((rows, cols), jnp.float32),
        ),
        scratch_shapes=[
            pltpu.VMEM((dim // 4, cols), jnp.float32),
            pltpu.VMEM(acts.shape, acts.dtype),
            pltpu.VMEM(cot.shape, cot.dtype),
            pltpu.VMEM(chosen.shape, chosen.dtype),
            pltpu.SemaphoreType.DMA,
            pltpu.SemaphoreType.DMA,
            pltpu.SemaphoreType.DMA,
        ],
        compiler_params=pltpu.CompilerParams(vmem_limit_bytes=40 << 20),
    )(in_hbm(acts), in_hbm(cot), in_hbm(chosen))


def encode_kernel(pieces_ref, moment_ref, mask_ref, table_ref, renewed_ref, copies_ref):
    moment_new = beta_decay * moment_ref[...] + jnp.sum(pieces_ref[...], axis=0)
    spectrum = jnp.dot(moment_new, table_ref[...], precision=highest, preferred_element_type=jnp.float32)
    retained = jnp.where(mask_ref[...] > 0.5, spectrum, 0.0)
    restored = lax.dot_general(
        retained, table_ref[...], (((1,), (1,)), ((), ())), precision=highest, preferred_element_type=jnp.float32
    )
    renewed_ref[...] = moment_new - restored
    copies_ref[...] = jnp.broadcast_to(restored, copies_ref.shape)


def encode(pieces, moment, mask, copies):
    rows, cols = moment.shape
    return pl.pallas_call(
        encode_kernel,
        out_shape=(
            jax.ShapeDtypeStruct((rows, cols), jnp.float32),
            jax.ShapeDtypeStruct((copies, rows, cols), jnp.float32),
        ),
        compiler_params=pltpu.CompilerParams(vmem_limit_bytes=16 << 20),
    )(pieces, moment, mask, jnp.asarray(span_tables(cols)))


def add_kernel(a_ref, b_ref, out_ref):
    out_ref[...] = a_ref[...] + b_ref[...]


def add(a, b):
    return pl.pallas_call(
        add_kernel,
        out_shape=jax.ShapeDtypeStruct(a.shape, a.dtype),
        compiler_params=pltpu.CompilerParams(vmem_limit_bytes=4 << 20),
        cost_estimate=pl.CostEstimate(flops=a.size, bytes_accessed=3 * a.nbytes, transcendentals=0),
    )(a, b)


def shards(activations, cotangent, momentum, components):
    groups = lax.axis_size("rep")
    away, near, kept_away, kept_near, mask = partials(
        activations[0], cotangent[0], components[0].transpose(1, 2, 0)
    )
    core = partners(lambda core: (0, 0, 1))
    once, twice = partners(lambda core: (core, 1 - core, 0)), partners(lambda core: (1 - core, core, 0))
    away = lax.ppermute(away, "fsdp", core)
    near = add(kept_near, lax.ppermute(near, "fsdp", core))
    two = lax.ppermute(kept_away[0] + away[0], "fsdp", once)
    one = lax.ppermute(kept_away[1] + away[1], "fsdp", once)
    here = add(near[1], one)
    mine = here + lax.ppermute(near[0] + two, "fsdp", twice)
    members = [
        [index_of(pair, group, x, core) for pair in range(PAIRS)]
        for group in range(2)
        for x in range(2)
        for core in range(2)
    ]
    pieces = lax.all_to_all(mine, "fsdp", 0, 0, axis_index_groups=members)
    renewed, copies = encode(pieces, momentum[0], mask, groups)
    restored = lax.all_to_all(copies, "rep", 0, 0)
    update = jnp.sum(restored, axis=0) / groups
    return (update, renewed[None])


def solution(mesh):
    return jax.shard_map(
        shards,
        mesh=mesh,
        in_specs=(
            P("rep", "fsdp", None),
            P("rep", "fsdp", None),
            P("rep", "fsdp", None),
            P("rep", "fsdp", None, None),
        ),
        out_specs=(P("fsdp", None), P("rep", "fsdp", None)),
        check_vma=False,
    )
```

```python
import math

import jax
import jax.numpy as jnp
import numpy as np
from jax import lax
from jax.experimental import pallas as pl
from jax.experimental.pallas import tpu as pltpu
from jax.sharding import PartitionSpec as P

SPAN = 64
PAIRS = 8
beta_decay = 0.999


def span_tables(cols):
    frequency = np.arange(SPAN, dtype=np.float64)[:, None]
    position = np.arange(SPAN, dtype=np.float64)[None, :]
    cosines = np.cos(math.pi * (2.0 * position + 1.0) * frequency / (2.0 * SPAN))
    cosines *= np.where(frequency == 0.0, math.sqrt(1.0 / SPAN), math.sqrt(2.0 / SPAN))
    return np.kron(np.eye(cols // SPAN), cosines.T).astype(np.float32)


def two_parts(table):
    high = table.astype(jnp.bfloat16)
    return np.stack([high, (table - high.astype(np.float32)).astype(jnp.bfloat16)])


def place(index):
    z = index // 4
    pair, bit = z // 2, z % 2
    return pair, bit ^ ((60 >> pair) & 1), (index // 2) % 2, index % 2


def index_of(pair, group, x, core):
    return (2 * pair + (group ^ ((60 >> pair) & 1))) * 4 + x * 2 + core


def partners(of):
    pairs = []
    for f in range(64):
        pair, group, x, core = place(f)
        dgroup, dx, dcore = of(core)
        pairs.append((f, index_of(pair, group ^ dgroup, x ^ dx, core ^ dcore)))
    return pairs


def in_hbm(array):
    return pltpu.with_memory_space_constraint(array, pltpu.HBM)


def partial_kernel(
    acts_hbm, cot_hbm, chosen_hbm, away_ref, near_ref, keep_away_ref, keep_near_ref, mask_ref, product, acts, cot, chosen_ref, acts_sem, cot_sem, chosen_sem
):
    copy_chosen = pltpu.make_async_copy(chosen_hbm, chosen_ref, chosen_sem)
    copy_chosen.start()
    copy_cot = pltpu.make_async_copy(cot_hbm, cot, cot_sem)
    copy_cot.start()
    half = acts.shape[1] // 2
    copies = [
        pltpu.make_async_copy(acts_hbm.at[:, pl.ds(at, half)], acts.at[:, pl.ds(at, half)], acts_sem.at[at // half])
        for at in (0, half)
    ]
    for copy in copies:
        copy.start()
    spans, kept, rows = chosen_ref.shape
    copy_chosen.wait()
    component = lax.broadcasted_iota(jnp.int32, (SPAN, rows), 0)
    masks = []
    for c in range(spans):
        hit = component == chosen_ref[c, 0:1, :]
        for j in range(1, kept):
            hit = hit | (component == chosen_ref[c, j : j + 1, :])
        masks.append(jnp.where(hit, 1.0, 0.0))
    mask_ref[...] = jnp.concatenate(masks, axis=0).T
    send_refs, keep_refs = (away_ref, near_ref), (keep_away_ref, keep_near_ref)
    _, group, x, core = place(lax.axis_index("fsdp"))
    copy_cot.wait()
    turned = cot[...].T
    width = acts.shape[1] // 4
    for step in range(4):
        if step % 2 == 0:
            copies[step // 2].wait()
        product[...] = jnp.dot(
            turned, acts[:, step * width : (step + 1) * width], preferred_element_type=jnp.float32
        ).T
        for local in range(width // (8 * rows)):
            pair = step * (width // (8 * rows)) + local
            for slot in range(4):
                early, late = 1 - slot // 2, 1 - slot % 2
                for to_core, at_core in ((core, keep_refs), (1 - core, send_refs)):
                    to_x = jnp.where(to_core == 0, early, late) ^ x
                    bit = jnp.where(to_core == 0, late, early) ^ group ^ ((60 >> pair) & 1)
                    at = (((local * 2 + bit) * 2 + to_x) * 2 + to_core) * rows
                    at_core[slot // 2][slot % 2, pair] = product[pl.ds(pl.multiple_of(at, 8), rows)]


def partials(acts, cot, chosen):
    dim, cols = acts.shape[1], cot.shape[1]
    rows = chosen.shape[2]
    return pl.pallas_call(
        partial_kernel,
        in_specs=[
            pl.BlockSpec(memory_space=pl.ANY),
            pl.BlockSpec(memory_space=pl.ANY),
            pl.BlockSpec(memory_space=pl.ANY),
        ],
        out_shape=(
            jax.ShapeDtypeStruct((2, PAIRS, rows, cols), jnp.float32),
            jax.ShapeDtypeStruct((2, PAIRS, rows, cols), jnp.float32),
            jax.ShapeDtypeStruct((2, PAIRS, rows, cols), jnp.float32),
            jax.ShapeDtypeStruct((2, PAIRS, rows, cols), jnp.float32),
            jax.ShapeDtypeStruct((rows, cols), jnp.float32),
        ),
        scratch_shapes=[
            pltpu.VMEM((dim // 4, cols), jnp.float32),
            pltpu.VMEM(acts.shape, acts.dtype),
            pltpu.VMEM(cot.shape, cot.dtype),
            pltpu.VMEM(chosen.shape, chosen.dtype),
            pltpu.SemaphoreType.DMA((2,)),
            pltpu.SemaphoreType.DMA,
            pltpu.SemaphoreType.DMA,
        ],
        compiler_params=pltpu.CompilerParams(vmem_limit_bytes=40 << 20),
    )(in_hbm(acts), in_hbm(cot), in_hbm(chosen))


def split(array):
    high = array.astype(jnp.bfloat16)
    return high, (array - high.astype(jnp.float32)).astype(jnp.bfloat16)


def product(array, table_ref, contract):
    high, low = split(array)
    rows = array.shape[0]
    dims = (((1,), (contract,)), ((), ()))
    both = lax.dot_general(
        jnp.concatenate([high, low]), table_ref[0], dims, preferred_element_type=jnp.float32
    )
    rest = lax.dot_general(high, table_ref[1], dims, preferred_element_type=jnp.float32)
    return both[:rows] + (both[rows:] + rest)


def encode_kernel(pieces_ref, moment_ref, mask_ref, table_ref, renewed_ref, copies_ref):
    moment_new = beta_decay * moment_ref[...] + jnp.sum(pieces_ref[...], axis=0)
    spectrum = product(moment_new, table_ref, 0)
    retained = jnp.where(mask_ref[...] > 0.5, spectrum, 0.0)
    restored = product(retained, table_ref, 1)
    renewed_ref[...] = moment_new - restored
    copies_ref[...] = jnp.broadcast_to(restored, copies_ref.shape)


def encode(pieces, moment, mask, copies):
    rows, cols = moment.shape
    return pl.pallas_call(
        encode_kernel,
        out_shape=(
            jax.ShapeDtypeStruct((rows, cols), jnp.float32),
            jax.ShapeDtypeStruct((copies, rows, cols), jnp.float32),
        ),
        compiler_params=pltpu.CompilerParams(vmem_limit_bytes=16 << 20),
    )(pieces, moment, mask, jnp.asarray(two_parts(span_tables(cols))))


def add_kernel(a_ref, b_ref, out_ref):
    out_ref[...] = a_ref[...] + b_ref[...]


def add(a, b):
    return pl.pallas_call(
        add_kernel,
        out_shape=jax.ShapeDtypeStruct(a.shape, a.dtype),
        compiler_params=pltpu.CompilerParams(vmem_limit_bytes=4 << 20),
        cost_estimate=pl.CostEstimate(flops=a.size, bytes_accessed=3 * a.nbytes, transcendentals=0),
    )(a, b)


def shards(activations, cotangent, momentum, components):
    groups = lax.axis_size("rep")
    away, near, kept_away, kept_near, mask = partials(
        activations[0], cotangent[0], components[0].transpose(1, 2, 0)
    )
    core = partners(lambda core: (0, 0, 1))
    once, twice = partners(lambda core: (core, 1 - core, 0)), partners(lambda core: (1 - core, core, 0))
    away = lax.ppermute(away, "fsdp", core)
    near = add(kept_near, lax.ppermute(near, "fsdp", core))
    two = lax.ppermute(kept_away[0] + away[0], "fsdp", once)
    one = lax.ppermute(kept_away[1] + away[1], "fsdp", once)
    here = add(near[1], one)
    mine = here + lax.ppermute(near[0] + two, "fsdp", twice)
    members = [
        [index_of(pair, group, x, core) for pair in range(PAIRS)]
        for group in range(2)
        for x in range(2)
        for core in range(2)
    ]
    pieces = lax.all_to_all(mine, "fsdp", 0, 0, axis_index_groups=members)
    renewed, copies = encode(pieces, momentum[0], mask, groups)
    restored = lax.all_to_all(copies, "rep", 0, 0)
    update = jnp.sum(restored, axis=0) / groups
    return (update, renewed[None])


def solution(mesh):
    return jax.shard_map(
        shards,
        mesh=mesh,
        in_specs=(
            P("rep", "fsdp", None),
            P("rep", "fsdp", None),
            P("rep", "fsdp", None),
            P("rep", "fsdp", None, None),
        ),
        out_specs=(P("fsdp", None), P("rep", "fsdp", None)),
        check_vma=False,
    )
```

```python
import math

import jax
import jax.numpy as jnp
import numpy as np
from jax import lax
from jax.experimental import pallas as pl
from jax.experimental.pallas import tpu as pltpu
from jax.sharding import PartitionSpec as P

SPAN = 64
PAIRS = 4
beta_decay = 0.999


def span_tables(cols):
    frequency = np.arange(SPAN, dtype=np.float64)[:, None]
    position = np.arange(SPAN, dtype=np.float64)[None, :]
    cosines = np.cos(math.pi * (2.0 * position + 1.0) * frequency / (2.0 * SPAN))
    cosines *= np.where(frequency == 0.0, math.sqrt(1.0 / SPAN), math.sqrt(2.0 / SPAN))
    return np.kron(np.eye(cols // SPAN), cosines.T).astype(np.float32)


def two_parts(table):
    high = table.astype(jnp.bfloat16)
    return np.stack([high, (table - high.astype(np.float32)).astype(jnp.bfloat16)])


def place(index):
    z = index // 4
    kind = ((z + 1) // 2) % 2
    pair = ((z + 16 - 3 + 2 * kind) % 16) // 4
    return pair, (1 - z % 2) ^ (pair // 2), kind, (index // 2) % 2, index % 2


def index_of(pair, side, kind, x, core):
    return ((4 * pair + 3 - 2 * kind + (side ^ (pair // 2))) % 16) * 4 + x * 2 + core


def neighbour(index, way):
    z, low = index // 4, index % 4
    if way == "core":
        return z * 4 + (low ^ 1)
    if way == "x":
        return z * 4 + (low ^ 2)
    if way == "across":
        return (z ^ 1) * 4 + low
    return ((z + 2 * (z % 2) + 15) % 16) * 4 + low


def partners(core_0, core_1):
    return [(f, neighbour(f, core_1 if f % 2 else core_0)) for f in range(64)]


def in_hbm(array):
    return pltpu.with_memory_space_constraint(array, pltpu.HBM)


def partial_kernel(
    acts_hbm, cot_hbm, chosen_hbm, away_ref, near_ref, keep_away_ref, keep_near_ref, mask_ref, product, acts, cot, chosen_ref, acts_sem, cot_sem, chosen_sem
):
    copy_chosen = pltpu.make_async_copy(chosen_hbm, chosen_ref, chosen_sem)
    copy_chosen.start()
    copy_cot = pltpu.make_async_copy(cot_hbm, cot, cot_sem)
    copy_cot.start()
    half = acts.shape[1] // 2
    copies = [
        pltpu.make_async_copy(acts_hbm.at[:, pl.ds(at, half)], acts.at[:, pl.ds(at, half)], acts_sem.at[at // half])
        for at in (0, half)
    ]
    for copy in copies:
        copy.start()
    spans, kept, rows = chosen_ref.shape
    copy_chosen.wait()
    component = lax.broadcasted_iota(jnp.int32, (SPAN, rows), 0)
    masks = []
    for c in range(spans):
        hit = component == chosen_ref[c, 0:1, :]
        for j in range(1, kept):
            hit = hit | (component == chosen_ref[c, j : j + 1, :])
        masks.append(jnp.where(hit, 1.0, 0.0))
    mask_ref[...] = jnp.concatenate(masks, axis=0).T
    me = lax.axis_index("fsdp")
    _, side, kind, x, core = place(me)
    _, side_across, _, _, _ = place((me // 4 ^ 1) * 4)
    copy_cot.wait()
    turned = cot[...].T
    width = acts.shape[1] // 4
    for step in range(4):
        if step % 2 == 0:
            copies[step // 2].wait()
        product[step * width : (step + 1) * width] = jnp.dot(
            turned, acts[:, step * width : (step + 1) * width], preferred_element_type=jnp.float32
        ).T
    for slot in range(8):
        first, second, third = 1 - slot // 4, 1 - slot // 2 % 2, 1 - slot % 2
        for to_core, refs in ((core, (keep_away_ref, keep_near_ref)), (1 - core, (away_ref, near_ref))):
            to_x = jnp.where(to_core == 0, first, third) ^ x
            across = jnp.where(to_core == 0, second, first)
            along = jnp.where(to_core == 0, third, second)
            to_side = along ^ jnp.where(across == 1, side_across, side)
            for pair in range(4):
                at = index_of(pair, to_side, kind ^ across, to_x, to_core) * rows
                refs[slot // 4][slot % 4, pair] = product[pl.ds(pl.multiple_of(at, 8), rows)]


def partials(acts, cot, chosen):
    dim, cols = acts.shape[1], cot.shape[1]
    rows = chosen.shape[2]
    return pl.pallas_call(
        partial_kernel,
        in_specs=[
            pl.BlockSpec(memory_space=pl.ANY),
            pl.BlockSpec(memory_space=pl.ANY),
            pl.BlockSpec(memory_space=pl.ANY),
        ],
        out_shape=(
            jax.ShapeDtypeStruct((4, PAIRS, rows, cols), jnp.float32),
            jax.ShapeDtypeStruct((4, PAIRS, rows, cols), jnp.float32),
            jax.ShapeDtypeStruct((4, PAIRS, rows, cols), jnp.float32),
            jax.ShapeDtypeStruct((4, PAIRS, rows, cols), jnp.float32),
            jax.ShapeDtypeStruct((rows, cols), jnp.float32),
        ),
        scratch_shapes=[
            pltpu.VMEM((dim, cols), jnp.float32),
            pltpu.VMEM(acts.shape, acts.dtype),
            pltpu.VMEM(cot.shape, cot.dtype),
            pltpu.VMEM(chosen.shape, chosen.dtype),
            pltpu.SemaphoreType.DMA((2,)),
            pltpu.SemaphoreType.DMA,
            pltpu.SemaphoreType.DMA,
        ],
        compiler_params=pltpu.CompilerParams(vmem_limit_bytes=40 << 20),
    )(in_hbm(acts), in_hbm(cot), in_hbm(chosen))


def split(array):
    high = array.astype(jnp.bfloat16)
    return high, (array - high.astype(jnp.float32)).astype(jnp.bfloat16)


def product(array, table_ref, contract):
    high, low = split(array)
    rows = array.shape[0]
    dims = (((1,), (contract,)), ((), ()))
    both = lax.dot_general(
        jnp.concatenate([high, low]), table_ref[0], dims, preferred_element_type=jnp.float32
    )
    rest = lax.dot_general(high, table_ref[1], dims, preferred_element_type=jnp.float32)
    return both[:rows] + (both[rows:] + rest)


def encode_kernel(pieces_ref, moment_ref, mask_ref, table_ref, renewed_ref, copies_ref):
    moment_new = beta_decay * moment_ref[...] + jnp.sum(pieces_ref[...], axis=0)
    spectrum = product(moment_new, table_ref, 0)
    retained = jnp.where(mask_ref[...] > 0.5, spectrum, 0.0)
    restored = product(retained, table_ref, 1)
    renewed_ref[...] = moment_new - restored
    copies_ref[...] = jnp.broadcast_to(restored, copies_ref.shape)


def encode(pieces, moment, mask, copies):
    rows, cols = moment.shape
    return pl.pallas_call(
        encode_kernel,
        out_shape=(
            jax.ShapeDtypeStruct((rows, cols), jnp.float32),
            jax.ShapeDtypeStruct((copies, rows, cols), jnp.float32),
        ),
        compiler_params=pltpu.CompilerParams(vmem_limit_bytes=16 << 20),
    )(pieces, moment, mask, jnp.asarray(two_parts(span_tables(cols))))


def add_kernel(a_ref, b_ref, out_ref):
    out_ref[...] = a_ref[...] + b_ref[...]


def add(a, b):
    return pl.pallas_call(
        add_kernel,
        out_shape=jax.ShapeDtypeStruct(a.shape, a.dtype),
        compiler_params=pltpu.CompilerParams(vmem_limit_bytes=4 << 20),
        cost_estimate=pl.CostEstimate(flops=a.size, bytes_accessed=3 * a.nbytes, transcendentals=0),
    )(a, b)


def shards(activations, cotangent, momentum, components):
    groups = lax.axis_size("rep")
    away, near, kept_away, kept_near, mask = partials(
        activations[0], cotangent[0], components[0].transpose(1, 2, 0)
    )
    core = partners("core", "core")
    move_1, move_2, move_3 = partners("x", "across"), partners("across", "along"), partners("along", "x")
    away = lax.ppermute(away, "fsdp", core)
    near = add(kept_near, lax.ppermute(near, "fsdp", core))
    two = lax.ppermute(kept_away[:2] + away[:2], "fsdp", move_1)
    one = lax.ppermute(kept_away[2:] + away[2:], "fsdp", move_1)
    here = add(near[2:], one)
    third = lax.ppermute(near[0] + two[0], "fsdp", move_2)
    none = lax.ppermute(near[1] + two[1], "fsdp", move_2)
    last = lax.ppermute(here[0] + third, "fsdp", move_3)
    mine = add(here[1], none) + last
    members = [
        [index_of(pair, side, kind, x, core) for pair in range(PAIRS)]
        for side in range(2)
        for kind in range(2)
        for x in range(2)
        for core in range(2)
    ]
    pieces = lax.all_to_all(mine, "fsdp", 0, 0, axis_index_groups=members)
    renewed, copies = encode(pieces, momentum[0], mask, groups)
    restored = lax.all_to_all(copies, "rep", 0, 0)
    update = jnp.sum(restored, axis=0) / groups
    return (update, renewed[None])


def solution(mesh):
    return jax.shard_map(
        shards,
        mesh=mesh,
        in_specs=(
            P("rep", "fsdp", None),
            P("rep", "fsdp", None),
            P("rep", "fsdp", None),
            P("rep", "fsdp", None, None),
        ),
        out_specs=(P("fsdp", None), P("rep", "fsdp", None)),
        check_vma=False,
    )
```

```python
import math

import jax
import jax.numpy as jnp
import numpy as np
from jax import lax
from jax.experimental import pallas as pl
from jax.experimental.pallas import tpu as pltpu
from jax.sharding import PartitionSpec as P

SPAN = 64
PAIRS = 4
beta_decay = 0.999


def span_tables(cols):
    frequency = np.arange(SPAN, dtype=np.float64)[:, None]
    position = np.arange(SPAN, dtype=np.float64)[None, :]
    cosines = np.cos(math.pi * (2.0 * position + 1.0) * frequency / (2.0 * SPAN))
    cosines *= np.where(frequency == 0.0, math.sqrt(1.0 / SPAN), math.sqrt(2.0 / SPAN))
    return np.kron(np.eye(cols // SPAN), cosines.T).astype(np.float32)


def two_parts(table):
    high = table.astype(jnp.bfloat16)
    return np.stack([high, (table - high.astype(np.float32)).astype(jnp.bfloat16)])


def place(index):
    z = index // 4
    kind = ((z + 1) // 2) % 2
    pair = ((z + 16 - 3 + 2 * kind) % 16) // 4
    return pair, (1 - z % 2) ^ (pair // 2), kind, (index // 2) % 2, index % 2


def index_of(pair, side, kind, x, core):
    return ((4 * pair + 3 - 2 * kind + (side ^ (pair // 2))) % 16) * 4 + x * 2 + core


def neighbour(index, way):
    z, low = index // 4, index % 4
    if way == "core":
        return z * 4 + (low ^ 1)
    if way == "x":
        return z * 4 + (low ^ 2)
    if way == "across":
        return (z ^ 1) * 4 + low
    return ((z + 2 * (z % 2) + 15) % 16) * 4 + low


def partners(core_0, core_1):
    return [(f, neighbour(f, core_1 if f % 2 else core_0)) for f in range(64)]


def in_hbm(array):
    return pltpu.with_memory_space_constraint(array, pltpu.HBM)


def partial_kernel(
    acts_hbm, cot_hbm, chosen_hbm, away_ref, near_ref, keep_away_ref, keep_near_ref, mask_ref, product, acts, cot, chosen_ref, acts_sem, cot_sem, chosen_sem
):
    copy_chosen = pltpu.make_async_copy(chosen_hbm, chosen_ref, chosen_sem)
    copy_chosen.start()
    copy_cot = pltpu.make_async_copy(cot_hbm, cot, cot_sem)
    copy_cot.start()
    half = acts.shape[1] // 2
    copies = [
        pltpu.make_async_copy(acts_hbm.at[:, pl.ds(at, half)], acts.at[:, pl.ds(at, half)], acts_sem.at[at // half])
        for at in (0, half)
    ]
    for copy in copies:
        copy.start()
    spans, kept, rows = chosen_ref.shape
    copy_chosen.wait()
    component = lax.broadcasted_iota(jnp.int32, (SPAN, rows), 0)
    masks = []
    for c in range(spans):
        hit = component == chosen_ref[c, 0:1, :]
        for j in range(1, kept):
            hit = hit | (component == chosen_ref[c, j : j + 1, :])
        masks.append(jnp.where(hit, 1.0, 0.0))
    mask_ref[...] = jnp.concatenate(masks, axis=0).T
    me = lax.axis_index("fsdp")
    _, side, kind, x, core = place(me)
    _, side_across, _, _, _ = place((me // 4 ^ 1) * 4)
    copy_cot.wait()
    turned = cot[...].T
    width = acts.shape[1] // 4
    for step in range(4):
        if step % 2 == 0:
            copies[step // 2].wait()
        product[step * width : (step + 1) * width] = jnp.dot(
            turned, acts[:, step * width : (step + 1) * width], preferred_element_type=jnp.float32
        ).T
    for slot in range(8):
        first, second, third = 1 - slot // 4, 1 - slot // 2 % 2, 1 - slot % 2
        for to_core, refs in ((core, (keep_away_ref, keep_near_ref)), (1 - core, (away_ref, near_ref))):
            to_x = jnp.where(to_core == 0, first, third) ^ x
            across = jnp.where(to_core == 0, second, first)
            along = jnp.where(to_core == 0, third, second)
            to_side = along ^ jnp.where(across == 1, side_across, side)
            for pair in range(4):
                at = index_of(pair, to_side, kind ^ across, to_x, to_core) * rows
                refs[slot // 4][slot % 4, pair] = product[pl.ds(pl.multiple_of(at, 8), rows)]


def partials(acts, cot, chosen):
    dim, cols = acts.shape[1], cot.shape[1]
    rows = chosen.shape[2]
    return pl.pallas_call(
        partial_kernel,
        in_specs=[
            pl.BlockSpec(memory_space=pl.ANY),
            pl.BlockSpec(memory_space=pl.ANY),
            pl.BlockSpec(memory_space=pl.ANY),
        ],
        out_shape=(
            jax.ShapeDtypeStruct((4, PAIRS, rows, cols), jnp.float32),
            jax.ShapeDtypeStruct((4, PAIRS, rows, cols), jnp.float32),
            jax.ShapeDtypeStruct((4, PAIRS, rows, cols), jnp.float32),
            jax.ShapeDtypeStruct((4, PAIRS, rows, cols), jnp.float32),
            jax.ShapeDtypeStruct((rows, cols), jnp.float32),
        ),
        scratch_shapes=[
            pltpu.VMEM((dim, cols), jnp.float32),
            pltpu.VMEM(acts.shape, acts.dtype),
            pltpu.VMEM(cot.shape, cot.dtype),
            pltpu.VMEM(chosen.shape, chosen.dtype),
            pltpu.SemaphoreType.DMA((2,)),
            pltpu.SemaphoreType.DMA,
            pltpu.SemaphoreType.DMA,
        ],
        compiler_params=pltpu.CompilerParams(vmem_limit_bytes=40 << 20),
    )(in_hbm(acts), in_hbm(cot), in_hbm(chosen))


def split(array):
    high = array.astype(jnp.bfloat16)
    return high, (array - high.astype(jnp.float32)).astype(jnp.bfloat16)


def product(array, table_ref, contract):
    high, low = split(array)
    rows = array.shape[0]
    dims = (((1,), (contract,)), ((), ()))
    both = lax.dot_general(
        jnp.concatenate([high, low]), table_ref[0], dims, preferred_element_type=jnp.float32
    )
    rest = lax.dot_general(high, table_ref[1], dims, preferred_element_type=jnp.float32)
    return both[:rows] + (both[rows:] + rest)


def encode_kernel(pieces_ref, moment_ref, mask_ref, table_ref, renewed_ref, copies_ref):
    moment_new = beta_decay * moment_ref[...] + jnp.sum(pieces_ref[...], axis=0)
    spectrum = product(moment_new, table_ref, 0)
    retained = jnp.where(mask_ref[...] > 0.5, spectrum, 0.0)
    restored = product(retained, table_ref, 1)
    renewed_ref[...] = moment_new - restored
    copies_ref[...] = jnp.broadcast_to(restored, copies_ref.shape)


def encode(pieces, moment, mask, copies):
    rows, cols = moment.shape
    return pl.pallas_call(
        encode_kernel,
        out_shape=(
            jax.ShapeDtypeStruct((rows, cols), jnp.float32),
            jax.ShapeDtypeStruct((copies, rows, cols), jnp.float32),
        ),
        compiler_params=pltpu.CompilerParams(vmem_limit_bytes=16 << 20),
    )(pieces, moment, mask, jnp.asarray(two_parts(span_tables(cols))))


def add_kernel(a_ref, b_ref, out_ref):
    out_ref[...] = a_ref[...] + b_ref[...]


def add(a, b):
    return pl.pallas_call(
        add_kernel,
        out_shape=jax.ShapeDtypeStruct(a.shape, a.dtype),
        compiler_params=pltpu.CompilerParams(vmem_limit_bytes=4 << 20),
        cost_estimate=pl.CostEstimate(flops=a.size, bytes_accessed=3 * a.nbytes, transcendentals=0),
    )(a, b)


def shards(activations, cotangent, momentum, components):
    groups = lax.axis_size("rep")
    away, near, kept_away, kept_near, mask = partials(
        activations[0], cotangent[0], components[0].transpose(1, 2, 0)
    )
    core = partners("core", "core")
    move_1, move_2, move_3 = partners("x", "across"), partners("across", "along"), partners("along", "x")
    away = lax.ppermute(away, "fsdp", core)
    near = add(kept_near, lax.ppermute(near, "fsdp", core))
    both = lax.ppermute(kept_away[0] + away[0], "fsdp", move_1)
    either = lax.ppermute(kept_away[1:3] + away[1:3], "fsdp", move_1)
    none = lax.ppermute(kept_away[3] + away[3], "fsdp", move_1)
    third = lax.ppermute(near[0] + both, "fsdp", move_2)
    here = add(near[2], either[1])
    ready = lax.ppermute(near[1] + either[0], "fsdp", move_2)
    last = lax.ppermute(here + third, "fsdp", move_3)
    mine = add(add(near[3], none), ready) + last
    members = [
        [index_of(pair, side, kind, x, core) for pair in range(PAIRS)]
        for side in range(2)
        for kind in range(2)
        for x in range(2)
        for core in range(2)
    ]
    pieces = lax.all_to_all(mine, "fsdp", 0, 0, axis_index_groups=members)
    renewed, copies = encode(pieces, momentum[0], mask, groups)
    restored = lax.all_to_all(copies, "rep", 0, 0)
    update = jnp.sum(restored, axis=0) / groups
    return (update, renewed[None])


def solution(mesh):
    return jax.shard_map(
        shards,
        mesh=mesh,
        in_specs=(
            P("rep", "fsdp", None),
            P("rep", "fsdp", None),
            P("rep", "fsdp", None),
            P("rep", "fsdp", None, None),
        ),
        out_specs=(P("fsdp", None), P("rep", "fsdp", None)),
        check_vma=False,
    )
```

```python
import math

import jax
import jax.numpy as jnp
import numpy as np
from jax import lax
from jax.experimental import pallas as pl
from jax.experimental.pallas import tpu as pltpu
from jax.sharding import PartitionSpec as P

SPAN = 64
PAIRS = 4
beta_decay = 0.999


def span_tables(cols):
    frequency = np.arange(SPAN, dtype=np.float64)[:, None]
    position = np.arange(SPAN, dtype=np.float64)[None, :]
    cosines = np.cos(math.pi * (2.0 * position + 1.0) * frequency / (2.0 * SPAN))
    cosines *= np.where(frequency == 0.0, math.sqrt(1.0 / SPAN), math.sqrt(2.0 / SPAN))
    return np.kron(np.eye(cols // SPAN), cosines.T).astype(np.float32)


def two_parts(table):
    high = table.astype(jnp.bfloat16)
    return np.stack([high, (table - high.astype(np.float32)).astype(jnp.bfloat16)])


def place(index):
    z = index // 4
    kind = ((z + 1) // 2) % 2
    pair = ((z + 16 - 3 + 2 * kind) % 16) // 4
    return pair, (1 - z % 2) ^ (pair // 2), kind, (index // 2) % 2, index % 2


def index_of(pair, side, kind, x, core):
    return ((4 * pair + 3 - 2 * kind + (side ^ (pair // 2))) % 16) * 4 + x * 2 + core


def neighbour(index, way):
    z, low = index // 4, index % 4
    if way == "core":
        return z * 4 + (low ^ 1)
    if way == "x":
        return z * 4 + (low ^ 2)
    if way == "across":
        return (z ^ 1) * 4 + low
    return ((z + 2 * (z % 2) + 15) % 16) * 4 + low


def partners(core_0, core_1):
    return [(f, neighbour(f, core_1 if f % 2 else core_0)) for f in range(64)]


def in_hbm(array):
    return pltpu.with_memory_space_constraint(array, pltpu.HBM)


def partial_kernel(
    acts_hbm, cot_hbm, chosen_hbm, away_ref, near_ref, keep_away_ref, keep_near_ref, mask_ref, product, acts, cot, chosen_ref, acts_sem, cot_sem, chosen_sem
):
    copy_chosen = pltpu.make_async_copy(chosen_hbm, chosen_ref, chosen_sem)
    copy_chosen.start()
    copy_cot = pltpu.make_async_copy(cot_hbm, cot, cot_sem)
    copy_cot.start()
    quarter, whole = acts.shape[1] // 4, acts.shape[1]
    copies = [
        pltpu.make_async_copy(acts_hbm.at[:, pl.ds(at, size)], acts.at[:, pl.ds(at, size)], acts_sem.at[number])
        for number, (at, size) in enumerate(((0, quarter), (quarter, whole - quarter)))
    ]
    for copy in copies:
        copy.start()
    spans, kept, rows = chosen_ref.shape
    copy_chosen.wait()
    component = lax.broadcasted_iota(jnp.int32, (SPAN, rows), 0)
    masks = []
    for c in range(spans):
        hit = component == chosen_ref[c, 0:1, :]
        for j in range(1, kept):
            hit = hit | (component == chosen_ref[c, j : j + 1, :])
        masks.append(jnp.where(hit, 1.0, 0.0))
    mask_ref[...] = jnp.concatenate(masks, axis=0).T
    me = lax.axis_index("fsdp")
    _, side, kind, x, core = place(me)
    _, side_across, _, _, _ = place((me // 4 ^ 1) * 4)
    copy_cot.wait()
    turned = cot[...].T
    width = acts.shape[1] // 4
    for step in range(4):
        if step < 2:
            copies[step].wait()
        product[step * width : (step + 1) * width] = jnp.dot(
            turned, acts[:, step * width : (step + 1) * width], preferred_element_type=jnp.float32
        ).T
    for slot in range(8):
        first, second, third = 1 - slot // 4, 1 - slot // 2 % 2, 1 - slot % 2
        for to_core, refs in ((core, (keep_away_ref, keep_near_ref)), (1 - core, (away_ref, near_ref))):
            to_x = jnp.where(to_core == 0, first, third) ^ x
            across = jnp.where(to_core == 0, second, first)
            along = jnp.where(to_core == 0, third, second)
            to_side = along ^ jnp.where(across == 1, side_across, side)
            for pair in range(4):
                at = index_of(pair, to_side, kind ^ across, to_x, to_core) * rows
                refs[slot // 4][slot % 4, pair] = product[pl.ds(pl.multiple_of(at, 8), rows)]


def partials(acts, cot, chosen):
    dim, cols = acts.shape[1], cot.shape[1]
    rows = chosen.shape[2]
    return pl.pallas_call(
        partial_kernel,
        in_specs=[
            pl.BlockSpec(memory_space=pl.ANY),
            pl.BlockSpec(memory_space=pl.ANY),
            pl.BlockSpec(memory_space=pl.ANY),
        ],
        out_shape=(
            jax.ShapeDtypeStruct((4, PAIRS, rows, cols), jnp.float32),
            jax.ShapeDtypeStruct((4, PAIRS, rows, cols), jnp.float32),
            jax.ShapeDtypeStruct((4, PAIRS, rows, cols), jnp.float32),
            jax.ShapeDtypeStruct((4, PAIRS, rows, cols), jnp.float32),
            jax.ShapeDtypeStruct((rows, cols), jnp.float32),
        ),
        scratch_shapes=[
            pltpu.VMEM((dim, cols), jnp.float32),
            pltpu.VMEM(acts.shape, acts.dtype),
            pltpu.VMEM(cot.shape, cot.dtype),
            pltpu.VMEM(chosen.shape, chosen.dtype),
            pltpu.SemaphoreType.DMA((2,)),
            pltpu.SemaphoreType.DMA,
            pltpu.SemaphoreType.DMA,
        ],
        compiler_params=pltpu.CompilerParams(vmem_limit_bytes=40 << 20),
    )(in_hbm(acts), in_hbm(cot), in_hbm(chosen))


def split(array):
    high = array.astype(jnp.bfloat16)
    return high, (array - high.astype(jnp.float32)).astype(jnp.bfloat16)


def product(array, table_ref, contract):
    high, low = split(array)
    rows = array.shape[0]
    dims = (((1,), (contract,)), ((), ()))
    both = lax.dot_general(
        jnp.concatenate([high, low]), table_ref[0], dims, preferred_element_type=jnp.float32
    )
    rest = lax.dot_general(high, table_ref[1], dims, preferred_element_type=jnp.float32)
    return both[:rows] + (both[rows:] + rest)


def encode_kernel(pieces_ref, moment_ref, mask_ref, table_ref, renewed_ref, copies_ref):
    moment_new = beta_decay * moment_ref[...] + jnp.sum(pieces_ref[...], axis=0)
    spectrum = product(moment_new, table_ref, 0)
    retained = jnp.where(mask_ref[...] > 0.5, spectrum, 0.0)
    restored = product(retained, table_ref, 1)
    renewed_ref[...] = moment_new - restored
    copies_ref[...] = jnp.broadcast_to(restored, copies_ref.shape)


def encode(pieces, moment, mask, copies):
    rows, cols = moment.shape
    return pl.pallas_call(
        encode_kernel,
        out_shape=(
            jax.ShapeDtypeStruct((rows, cols), jnp.float32),
            jax.ShapeDtypeStruct((copies, rows, cols), jnp.float32),
        ),
        compiler_params=pltpu.CompilerParams(vmem_limit_bytes=16 << 20),
    )(pieces, moment, mask, jnp.asarray(two_parts(span_tables(cols))))


def add_kernel(a_ref, b_ref, out_ref):
    out_ref[...] = a_ref[...] + b_ref[...]


def add(a, b):
    return pl.pallas_call(
        add_kernel,
        out_shape=jax.ShapeDtypeStruct(a.shape, a.dtype),
        compiler_params=pltpu.CompilerParams(vmem_limit_bytes=4 << 20),
        cost_estimate=pl.CostEstimate(flops=a.size, bytes_accessed=3 * a.nbytes, transcendentals=0),
    )(a, b)


def shards(activations, cotangent, momentum, components):
    groups = lax.axis_size("rep")
    away, near, kept_away, kept_near, mask = partials(
        activations[0], cotangent[0], components[0].transpose(1, 2, 0)
    )
    core = partners("core", "core")
    move_1, move_2, move_3 = partners("x", "across"), partners("across", "along"), partners("along", "x")
    away = lax.ppermute(away, "fsdp", core)
    near = add(kept_near, lax.ppermute(near, "fsdp", core))
    both = lax.ppermute(kept_away[0] + away[0], "fsdp", move_1)
    either = lax.ppermute(kept_away[1:3] + away[1:3], "fsdp", move_1)
    none = lax.ppermute(kept_away[3] + away[3], "fsdp", move_1)
    third = lax.ppermute(near[0] + both, "fsdp", move_2)
    here = add(near[2], either[1])
    ready = lax.ppermute(near[1] + either[0], "fsdp", move_2)
    last = lax.ppermute(here + third, "fsdp", move_3)
    mine = add(add(near[3], none), ready) + last
    members = [
        [index_of(pair, side, kind, x, core) for pair in range(PAIRS)]
        for side in range(2)
        for kind in range(2)
        for x in range(2)
        for core in range(2)
    ]
    pieces = lax.all_to_all(mine, "fsdp", 0, 0, axis_index_groups=members)
    renewed, copies = encode(pieces, momentum[0], mask, groups)
    restored = lax.all_to_all(copies, "rep", 0, 0)
    update = jnp.sum(restored, axis=0) / groups
    return (update, renewed[None])


def solution(mesh):
    return jax.shard_map(
        shards,
        mesh=mesh,
        in_specs=(
            P("rep", "fsdp", None),
            P("rep", "fsdp", None),
            P("rep", "fsdp", None),
            P("rep", "fsdp", None, None),
        ),
        out_specs=(P("fsdp", None), P("rep", "fsdp", None)),
        check_vma=False,
    )
```
